128 devices in a mesh: replica: 16 (over z, x_lo, core), mp: 8 (over x_hi, y).
Axes of the slice: x: 4 (x_hi: 2, x_lo: 2; x = x_hi * 2 + x_lo), y: 4, z: 4, core: 2. Of those that a mesh axis runs over, the one named last changes fastest.
Arguments:
- hidden: bfloat16 [8192, 7168], P('replica', 'mp'), may hold values from -6 to 6
- inner_down: bfloat16 [16, 7168, 4096], P('replica', 'mp'), may hold values from -6 to 6
- residual_in: bfloat16 [8192, 4096], P(('replica', 'mp')), may hold values from -120 to 120
- gain: float32 [4096], replicated, may hold values from 0.25 to 1.75
- cotangent: bfloat16 [8192, 4096], P(('replica', 'mp')), may hold values from -6 to 6
- codes: bfloat16 [16, 4096, 4096], P('replica', 'mp'), may hold values from -448 to 448, as said below
- scales: float32 [16, 4096, 32], P('replica', 'mp'), may hold values from 0.005 to 0.06
- outer_params: float32 [4096, 4096], P('mp', 'replica'), may hold values from -6 to 6
- momentum: float32 [4096, 4096], P('mp', 'replica'), may hold values from -1.8 to 1.8
Outputs:
- normed: bfloat16 [8192, 4096], P(('replica', 'mp'))
- grad_hidden: bfloat16 [8192, 7168], P('replica', 'mp')
- grad_gain: float32 [16, 4096], P('replica')
- new_params: float32 [4096, 4096], P('mp', 'replica')
- new_momentum: float32 [4096, 4096], P('mp', 'replica')
- merged: bfloat16 [16, 4096, 4096], P('replica', 'mp')
The draws below stay inside these ranges and needn't reach their ends.
Inputs may be any that keep to these rules, and one draw needn't show every extreme that they name: `codes`: every entry is a value of the e4m3 eight-bit float format (three mantissa bits), at most 448 in magnitude.
All inputs are finite; a program needn't handle non-finite values.
Results may differ from the reference program's by a relative error of at most 0.022.
Values may be sent and summed in bfloat16 or wider, within the bound.
A program may use at most 128 MiB of HBM per device.

```python
import math
import jax
import jax.numpy as jnp
from jax import lax

D = 4096
FF = 7168
BLOCK = 128
TOK = 512
FRAG_ROWS = 512
UNIT_BLOCK = 896
FRAG = 4096
REPLICAS = 16
TOKENS = 8192
N_MP = 8


def draw_codes(key, part):
    key = jax.random.fold_in(key, 11)
    subkeys = jax.random.split(key, 5)
    layout = (REPLICAS, FRAG, D)
    sign_bit = jax.random.randint(subkeys[0], layout, 0, 2)
    exponent = jnp.maximum(jax.random.randint(subkeys[1], layout, 1, 16), jax.random.randint(subkeys[2], layout, 1, 16))
    exponent = jnp.maximum(exponent, jax.random.randint(subkeys[3], layout, 1, 16))
    mantissa = jax.random.randint(subkeys[4], layout, 0, 8)
    mantissa = jnp.where((exponent == 15) & (mantissa == 7), 6, mantissa)
    magnitude = jnp.left_shift(jnp.ones(layout, jnp.int32), exponent).astype(jnp.float32) / 128.0
    values = (1 - 2 * sign_bit).astype(jnp.float32) * (1.0 + mantissa.astype(jnp.float32) / 8.0) * magnitude
    return values.astype(jnp.bfloat16)


def draw_residual_in(key, part):
    key = jax.random.fold_in(key, 23)
    subkeys = jax.random.split(key, 3)
    row_scale = jnp.exp(jax.random.uniform(subkeys[0], (TOKENS, 1), jnp.float32, 0.0, 2.3))
    column_scale = jnp.exp(jax.random.uniform(subkeys[1], (1, D), jnp.float32, 0.0, 2.3))
    noise = jax.random.truncated_normal(subkeys[2], -4.0, 4.0, (TOKENS, D), jnp.float32)
    return (0.3 * noise * row_scale * column_scale).astype(jnp.bfloat16)


def block_levels(key, shape, cuts, smallest, top_value):
    level, own = 1.0, jax.random.fold_in(key, 6)
    for position, blocks in cuts:
        heights = jnp.exp(jax.random.uniform(jax.random.fold_in(own, position), (blocks,), jnp.float32, smallest / len(cuts), top_value / len(cuts)))
        level = level * jnp.repeat(heights, shape[position] // blocks).reshape([-1 if axis == position else 1 for axis in range(len(shape))])
    return level


def centred(stream_key, extent, spread, bound, pieces=(), held_as=jnp.bfloat16):
    loudness = block_levels(stream_key, extent, pieces, -0.22, 0.18) if pieces else 1.0
    result = jax.random.normal(stream_key, extent, jnp.float32) * spread * loudness
    return jnp.minimum(jnp.maximum(result, -bound), bound).astype(held_as)


def setup_inputs(seed: int = 0) -> dict:
    arg_keys = jax.random.split(jax.random.key(seed), 10)
    return {
        "hidden": centred(arg_keys[0], (TOKENS, FF), 1.0, 6.0, ((0, 16), (1, 8))),
        "inner_down": centred(arg_keys[1], (REPLICAS, FF, D), 1.0, 6.0, ((0, 16), (1, 8))),
        "residual_in": draw_residual_in(jax.random.fold_in(arg_keys[9], 71), 0),
        "gain": jnp.clip(1.0 + 0.15 * jax.random.normal(arg_keys[3], (D,), jnp.float32), 0.25, 1.75),
        "cotangent": centred(arg_keys[4], (TOKENS, D), 1.0, 6.0, ((0, 128),)),
        "codes": draw_codes(jax.random.fold_in(arg_keys[9], 71), 0),
        "scales": jnp.clip(jnp.exp(math.log(0.06) - 2.4849066 * jax.random.uniform(arg_keys[6], (REPLICAS, FRAG, D // BLOCK), jnp.float32) ** block_levels(arg_keys[6], (REPLICAS, FRAG, D // BLOCK), ((0, 16), (1, 8)), -0.2, 0.2)), 0.005, 0.06),
        "outer_params": centred(arg_keys[7], (FRAG, D), 1.0, 6.0, ((0, 8), (1, 16)), jnp.float32),
        "momentum": centred(arg_keys[8], (FRAG, D), 0.3, 1.8, ((0, 8), (1, 16)), jnp.float32),
    }


momentum_rate = 0.9
outer_rate = 0.7
mix_rate = 0.5

def replica_step(inputs):
    hid_rows, weights, resid_rows, cot_rows, gain = inputs
    blocks_h = hid_rows.astype(jnp.float32).reshape(TOK, N_MP, UNIT_BLOCK)
    blocks_w = weights.astype(jnp.float32).reshape(N_MP, UNIT_BLOCK, D)
    partials = jnp.einsum('tku,kud->ktd', blocks_h, blocks_w, precision=lax.Precision.HIGHEST) * FF ** (-0.5)
    partials = lax.optimization_barrier(partials.astype(jnp.bfloat16)).astype(jnp.float32)
    mixed = resid_rows.astype(jnp.float32) + lax.optimization_barrier(jnp.sum(partials, 0))
    inv_rms = lax.rsqrt(lax.optimization_barrier(jnp.mean(mixed * mixed, -1, keepdims=True)) + 1e-05)
    unit_rows = mixed * inv_rms
    normed = (unit_rows * gain).astype(jnp.bfloat16)
    cot_float = cot_rows.astype(jnp.float32)
    grad_gain = lax.optimization_barrier(jnp.sum(cot_float * unit_rows, 0))
    scaled = cot_float * gain
    grad_mixed = (inv_rms * (scaled - unit_rows * lax.optimization_barrier(jnp.mean(scaled * unit_rows, -1, keepdims=True)))).astype(jnp.bfloat16)
    grad_hidden = lax.dot_general(grad_mixed, weights, (((1,), (1,)), ((), ())), preferred_element_type=jnp.float32)
    grad_hidden = (grad_hidden * FF ** (-0.5)).astype(jnp.bfloat16)
    fragment = weights.reshape(N_MP, UNIT_BLOCK, D)[:, :FRAG_ROWS].reshape(FRAG, D)
    return (normed, grad_hidden, grad_gain, fragment)

def add_replica(summed_all, replica_item):
    code_rows, scale_rows = replica_item
    decoded = code_rows.astype(jnp.float32).reshape(FRAG, D // BLOCK, BLOCK) * scale_rows[..., None]
    return (summed_all + decoded.reshape(FRAG, D), None)

def reference(hidden, inner_down, residual_in, gain, cotangent, codes, scales, outer_params, momentum):
    gains = jnp.broadcast_to(gain, (REPLICAS, D))
    normed, grad_hidden, grad_gain, fragment = lax.map(replica_step, (hidden.reshape(REPLICAS, TOK, FF), inner_down, residual_in.reshape(REPLICAS, TOK, D), cotangent.reshape(REPLICAS, TOK, D), gains))
    summed_all, _ = lax.scan(add_replica, jnp.zeros((FRAG, D), jnp.float32), (codes, scales))
    outer_step = summed_all / REPLICAS
    new_momentum = momentum_rate * momentum + outer_step
    new_params = outer_params - outer_rate * (outer_step + momentum_rate * new_momentum)
    fresh = lax.optimization_barrier(new_params.astype(jnp.bfloat16))
    merged = (mix_rate * fragment.astype(jnp.float32) + (1.0 - mix_rate) * fresh.astype(jnp.float32)[None]).astype(jnp.bfloat16)
    return (normed.reshape(TOKENS, D), grad_hidden.reshape(TOKENS, FF), grad_gain, new_params, new_momentum, merged)
```

```python
import functools

import jax
import jax.numpy as jnp
from jax import lax
from jax.experimental import pallas as pl
from jax.experimental.pallas import tpu as pltpu
from jax.sharding import PartitionSpec as P

FF = 7168
BLOCK = 128
MESH = pl.DeviceIdType.MESH

momentum_rate = 0.9
outer_rate = 0.7
mix_rate = 0.5

D = 4096
UNITS = 896
ROWS = 16
CHUNKS = 4
PARTS = 2
FRAG_ROWS = 512
PART = FRAG_ROWS // PARTS
SHARE = 256
HALF = D // 2
X_FIRST = (False, True, False, False)
CUT = 512
PLACE_ROWS = 128
N_SEND, N_RECV, N_LOCAL = 160, 160, 40

SCHEDULE = (
    ("mm1", 0), ("dec", 0), ("mm1", 1), ("mm1", 2), ("zs", 0), ("mid", 0), ("mm1", 3), ("dec", 1),
    ("zm", 0), ("zs", 1), ("mid", 2), ("ze", 0), ("xadd", 1), ("end", 0), ("zm", 1), ("mid", 3),
    ("up", 0), ("ze", 1), ("norm", 0), ("end", 2), ("mid", 1), ("bp", 0), ("up", 1), ("end", 3),
    ("bf", 0), ("agp", 0), ("end", 1), ("norm", 1), ("norm", 2), ("agf", 0), ("bc", 0), ("bp", 1),
    ("mg", 0), ("norm", 3), ("gg", 0), ("agf", 1), ("bf", 1), ("agx", 0), ("agp", 2), ("gg", 1),
    ("mm2", 0), ("bc", 1), ("agp", 3), ("agx", 1), ("mm3", 0), ("gg", 2), ("mg", 1), ("agf", 2),
    ("agf", 3), ("mm2", 1), ("agx", 2), ("gg", 3), ("mm2", 2), ("mm3", 1), ("agx", 3), ("mm2", 3),
    ("mm3", 3), ("mm3", 2),
)


class Ring:
    def __init__(self, kit, pos, nxt, prv):
        self.kit, self.pos, self.nxt, self.prv = kit, pos, nxt, prv

    def at(self, step):
        return lax.rem(self.pos + (step % 4), 4)

    def scatter(self, piece, fwd, own, total):
        kit = self.kit
        self.piece, self.fwd, self.own, self.total = piece, fwd, own, total
        two = self.at(2)
        self.got_fwd = (
            kit.send(piece(two, 0), fwd(0), self.nxt),
            kit.send(piece(two, 1), fwd(1), self.prv),
        )
        got_right = kit.send(piece(self.at(1), 1), own(1), self.nxt)
        got_left = kit.send(piece(self.at(3), 0), own(0), self.prv)
        self.got_own = (got_left, got_right)

    def middle(self):
        kit, out = self.kit, []
        for k, (step, to) in enumerate(((1, self.nxt), (3, self.prv))):
            self.got_fwd[k].wait_recv()
            mine = self.piece(self.at(step), k)
            add_into(mine, self.fwd(k))
            out.append(kit.send(mine, self.total(k), to))
        self.got_total = out

    def finish(self):
        for k in range(2):
            self.got_own[k].wait_recv()
            self.got_total[k].wait_recv()

    def gather_open(self, slot):
        self.slot = slot
        self.base = [self.kit.recv_slots(2), self.kit.recv_slots(2)]

    def gather(self, k):
        kit, mine = self.kit, self.slot(self.pos, k)
        kit.send(mine, mine, self.nxt, self.base[0] + k)
        kit.send(mine, mine, self.prv, self.base[1] + k)

    def await_near(self, way, k):
        there = self.slot(self.at(3 if way == 0 else 1), k)
        self.kit.wait_on(there, self.base[way] + k)

    def forward(self):
        kit = self.kit
        self.far = []
        for k, (step, to) in enumerate(((3, self.nxt), (1, self.prv))):
            self.await_near(k, k)
            there = self.slot(self.at(step), k)
            index = kit.recv_slots(1)
            kit.send(there, there, to, index)
            self.far.append(index)

    def await_rest(self):
        self.await_near(0, 1)
        self.await_near(1, 0)

    def await_far(self):
        for k in range(2):
            self.kit.wait_on(self.slot(self.at(2), k), self.far[k])


class Kit:
    def __init__(self, ssem, rsem, lsem):
        self.ssem, self.rsem, self.lsem = ssem, rsem, lsem
        self.sends, self.recvs, self.locals = 0, 0, 0
        self.open = []

    def recv_slots(self, n):
        self.recvs += n
        assert self.recvs <= N_RECV
        return self.recvs - n

    def send(self, src, dst, to, index=None):
        if index is None:
            index = self.recv_slots(1)
        copy = pltpu.make_async_remote_copy(
            src_ref=src,
            dst_ref=dst,
            send_sem=self.ssem.at[self.sends],
            recv_sem=self.rsem.at[index],
            device_id=to,
            device_id_type=MESH,
        )
        self.sends += 1
        assert self.sends <= N_SEND
        copy.start()
        self.open.append(copy.wait_send)
        return copy

    def wait_on(self, ref, index):
        pltpu.make_async_copy(ref, ref, self.rsem.at[index]).wait()

    def local(self, src, dst):
        copy = pltpu.make_async_copy(src, dst, self.lsem.at[self.locals])
        self.locals += 1
        assert self.locals <= N_LOCAL
        copy.start()
        return copy

    def out(self, src, dst):
        self.open.append(self.local(src, dst).wait)


def f32(value):
    return value.astype(jnp.float32)


def add_into(a, b):
    a[...] = (f32(a[...]) + f32(b[...])).astype(jnp.bfloat16)


def sync_kernel(
    hidden, weights, resid, gain, cot, codes, scales, params, mom,
    normed_o, hgrad_o, ggain_o, params_o, mom_o, merged_o,
    w, hid, lhs, prod, a_fwd, a_own, a_sum, a_x, a_x4, gm, res, ct, gn, mixed, nrm, hg, gg, gs, gr,
    cd, sc, dec, core_in, b_fwd, b_own, b_sum, b_x, fresh, pr, mo,
    ssem, rsem, lsem,
):
    kit = Kit(ssem, rsem, lsem)
    r, m = lax.axis_index("replica"), lax.axis_index("mp")
    z, xl, c = r // 4, lax.rem(r // 2, 2), lax.rem(r, 2)
    xh, y = m // 4, lax.rem(m, 4)

    def place(z, xl, c, xh, y):
        return (z * 4 + xl * 2 + c, xh * 4 + y)

    y_next, y_prev = place(z, xl, c, xh, lax.rem(y + 1, 4)), place(z, xl, c, xh, lax.rem(y + 3, 4))
    z_next, z_prev = place(lax.rem(z + 1, 4), xl, c, xh, y), place(lax.rem(z + 3, 4), xl, c, xh, y)
    x_far, x_near, other = place(z, xl, c, 1 - xh, y), place(z, 1 - xl, c, xh, y), place(z, xl, 1 - c, xh, y)

    load_hid = kit.local(hidden, hid)
    width = D // 4
    load_w = [
        kit.local(weights.at[:, pl.ds(i * width, width)], w.at[:, pl.ds(i * width, width)])
        for i in range(4)
    ]
    loads = {}

    def load_rest():
        loads["sc"] = kit.local(scales, sc)
        for i in range(PARTS):
            rows = pl.ds(i * PART, PART)
            loads["cd", i] = kit.local(codes.at[rows], cd.at[rows])
        loads["norm"] = [kit.local(resid, res), kit.local(cot, ct), kit.local(gain, gn)]
        loads["outer"] = [kit.local(params, pr), kit.local(mom, mo)]

    barrier = pltpu.get_barrier_semaphore()
    peers = (y_next, y_prev, z_next, z_prev, x_far, x_near, other)
    for peer in peers:
        pl.semaphore_signal(barrier, inc=1, device_id=peer, device_id_type=MESH)

    scale_ff = FF ** (-0.5)
    ring_a = [Ring(kit, y, y_next, y_prev) for _ in range(CHUNKS)]
    ring_b = [Ring(kit, z, z_next, z_prev) for _ in range(PARTS)]
    state = {}
    load_hid.wait()

    def half(k):
        return pl.ds(k * HALF, HALF)

    def ring_start(i):
        if X_FIRST[i]:
            ring_a[i].scatter(
                lambda pos, k: prod.at[i, pos, xh, :, half(k)],
                lambda k: a_fwd.at[i, 0, :, half(k)],
                lambda k: a_own.at[i, 0, :, half(k)],
                lambda k: a_sum.at[i, 0, :, half(k)],
            )
        else:
            ring_a[i].scatter(
                lambda pos, k: prod.at[i, pos, k],
                lambda k: a_fwd.at[i, k],
                lambda k: a_own.at[i, k],
                lambda k: a_sum.at[i, k],
            )

    def mm1(i):
        for yy in range(4):
            for xx in range(2):
                lhs[pl.ds((yy * 2 + xx) * ROWS, ROWS), :] = hid[
                    pl.ds((xx * 4 + yy) * 64 + i * ROWS, ROWS), :
                ]
        for q in range(4):
            if i == 0:
                load_w[q].wait()
            cols = pl.ds(q * width, width)
            out = jnp.dot(lhs[...], w[:, cols], preferred_element_type=jnp.float32)
            out = (out * scale_ff).astype(jnp.bfloat16)
            prod[i, :, :, :, cols] = out.reshape(4, 2, ROWS, width)
        if i == 0:
            load_rest()
            pl.semaphore_wait(barrier, len(peers))

        if X_FIRST[i]:
            state["x4", i] = kit.send(prod.at[i, :, 1 - xh], a_x4, x_far)
        else:
            ring_start(i)

    def xadd(i):
        if not X_FIRST[i]:
            return
        state["x4", i].wait_recv()
        for pos in range(4):
            add_into(prod.at[i, pos, xh], a_x4.at[pos])
        ring_start(i)

    def mid(i):
        ring_a[i].middle()

    def end(i):
        ring_a[i].finish()
        if X_FIRST[i]:
            return
        k = 1 - xh
        gone = prod.at[i, y, k]
        gone[...] = (f32(gone[...]) + f32(a_own[i, k]) + f32(a_sum[i, k])).astype(jnp.bfloat16)
        state["x", i] = kit.send(gone, a_x.at[i], x_far)

    def norm(i):
        if i == 0:
            for load in loads["norm"]:
                load.wait()
        if not X_FIRST[i]:
            state["x", i].wait_recv()
        rows = pl.ds(i * ROWS, ROWS)
        step = D // 4
        square = jnp.zeros((ROWS, 1), jnp.float32)
        for q in range(4):
            cols = pl.ds(q * step, step)
            if X_FIRST[i]:
                terms = (prod[i, y, xh, :, cols], a_own[i, 0, :, cols], a_sum[i, 0, :, cols])
            else:
                terms = (prod[i, y, xh, :, cols], a_own[i, xh, :, cols], a_sum[i, xh, :, cols], a_x[i, :, cols])
            value = f32(res[rows, cols])
            for term in terms:
                value = value + f32(term)
            mixed[:, cols] = value
            square = square + jnp.sum(value * value, -1, keepdims=True)
        inv = lax.rsqrt(square / D + 1e-05)
        along = jnp.zeros((ROWS, 1), jnp.float32)
        for q in range(4):
            cols = pl.ds(q * step, step)
            unit = mixed[:, cols] * inv
            mixed[:, cols] = unit
            gain_row = gn[:, cols]
            nrm[rows, cols] = (unit * gain_row).astype(jnp.bfloat16)
            cot_rows = f32(ct[rows, cols])
            along = along + jnp.sum(cot_rows * gain_row * unit, -1, keepdims=True)
            pair = cot_rows * unit
            pair = pair[:8] + pair[8:]
            if i == 0:
                gg[:, cols] = pair
            else:
                gg[:, cols] += pair
        along = along / D
        for q in range(4):
            cols = pl.ds(q * step, step)
            scaled = f32(ct[rows, cols]) * gn[:, cols]
            gm[i, y, xh, :, cols] = (inv * (scaled - mixed[:, cols] * along)).astype(jnp.bfloat16)
        if X_FIRST[i]:
            ring_a[i].gather_open(lambda pos, k: gm.at[i, pos, xh, :, half(k)])
            ring_a[i].gather(0)
            ring_a[i].gather(1)
            state["gx", i] = kit.recv_slots(4)
            mine = gm.at[i, y, xh]
            kit.send(mine, mine, x_far, state["gx", i] + y)
        else:
            ring_a[i].gather_open(lambda pos, k: gm.at[i, pos, k])
            mine = gm.at[i, y, xh]
            state["gx", i] = kit.recv_slots(1)
            kit.send(mine, mine, x_far, state["gx", i])
            ring_a[i].gather(xh)
        if i == CHUNKS - 1:
            kit.out(nrm, normed_o)

    def agp(i):
        if not X_FIRST[i]:
            kit.wait_on(gm.at[i, y, 1 - xh], state["gx", i])
            ring_a[i].gather(1 - xh)

    def agf(i):
        ring = ring_a[i]
        ring.forward()
        ring.await_rest()
        if X_FIRST[i]:
            for step in (1, 3):
                there = gm.at[i, ring.at(step), xh]
                kit.send(there, there, x_far, state["gx", i] + ring.at(step))

    def agx(i):
        ring = ring_a[i]
        ring.await_far()
        if X_FIRST[i]:
            there = gm.at[i, ring.at(2), xh]
            kit.send(there, there, x_far, state["gx", i] + ring.at(2))

    def back(i, first, count):
        units = pl.ds(first, count)
        out = lax.dot_general(
            w[units, :],
            gm[i].reshape(8 * ROWS, D),
            (((1,), (1,)), ((), ())),
            preferred_element_type=jnp.float32,
        )
        out = (out * scale_ff).T.astype(jnp.bfloat16)
        for yy in range(4):
            for xx in range(2):
                at = (yy * 2 + xx) * ROWS
                hg[pl.ds((xx * 4 + yy) * 64 + i * ROWS, ROWS), units] = out[at : at + ROWS]
        state["hg"] = state.get("hg", 0) + 1
        if state["hg"] == 2 * CHUNKS:
            kit.out(hg, hgrad_o)

    def mm2(i):
        if X_FIRST[i]:
            for pos in range(4):
                kit.wait_on(gm.at[i, pos, 1 - xh], state["gx", i] + pos)
        back(i, 0, CUT)

    def mm3(i):
        back(i, CUT, UNITS - CUT)

    def gain_sum(step):
        partner = (x_far, None, None)[step] if step < 1 else None
        if step == 0:
            gs[0] = jnp.sum(gg[...], 0, keepdims=True)
        elif step < 4:
            state["gg", step - 1].wait_recv()
            gs[step] = gs[step - 1] + gr[step - 1]
        if step == 1:
            partner = place(z, xl, c, xh, y + 1 - 2 * lax.rem(y, 2))
        if step == 2:
            partner = place(z, xl, c, xh, 3 - y)
        if step < 3:
            state["gg", step] = kit.send(gs.at[step], gr.at[step], partner)
        else:
            kit.out(gs.at[3], ggain_o)

    def decode(k):
        if k == 0:
            loads["sc"].wait()
        loads["cd", k].wait()
        rows = pl.ds(k * PART, PART)
        factors = sc[:, rows].T
        for j in range(D // BLOCK):
            target, part = j // 2, j % 2
            value = f32(cd[rows, pl.ds(j * BLOCK, BLOCK)]) * factors[:, j : j + 1]
            dec[k, target % 2, target // 4, (target // 2) % 2, :, pl.ds(part * BLOCK, BLOCK)] = value.astype(
                jnp.bfloat16
            )
        state["core", k] = kit.send(dec.at[k, 1 - c], core_in.at[k], other)

    def zs(k):
        state["core", k].wait_recv()
        for step in (2, 1, 3, 0):
            at = ring_b[k].at(step)
            for way in range(2):
                add_into(dec.at[k, c, at, way], core_in.at[k, at, way])
        ring_b[k].scatter(
            lambda pos, way: dec.at[k, c, pos, way],
            lambda way: b_fwd.at[k, way],
            lambda way: b_own.at[k, way],
            lambda way: b_sum.at[k, way],
        )

    def zm(k):
        ring_b[k].middle()

    def ze(k):
        ring_b[k].finish()
        way = 1 - xl
        gone = dec.at[k, c, z, way]
        gone[...] = (f32(gone[...]) + f32(b_own[k, way]) + f32(b_sum[k, way])).astype(jnp.bfloat16)
        state["xl", k] = kit.send(gone, b_x.at[k], x_near)

    def update(k):
        if k == 0:
            for load in loads["outer"]:
                load.wait()
        state["xl", k].wait_recv()
        rows = pl.ds(k * PART, PART)
        total = f32(dec[k, c, z, xl]) + f32(b_own[k, xl]) + f32(b_sum[k, xl]) + f32(b_x[k])
        step = total / 16
        new_mom = momentum_rate * mo[rows, :] + step
        new_params = pr[rows, :] - outer_rate * (step + momentum_rate * new_mom)
        mo[rows, :] = new_mom
        pr[rows, :] = new_params
        mine = fresh.at[k, c, z, xl]
        mine[...] = new_params.astype(jnp.bfloat16)
        ring_b[k].gather_open(lambda pos, way: fresh.at[k, c, pos, way])
        state["fx", k] = kit.recv_slots(1)
        kit.send(mine, mine, x_near, state["fx", k])
        ring_b[k].gather(xl)
        kit.out(mo.at[rows], mom_o.at[rows])
        kit.out(pr.at[rows], params_o.at[rows])

    def bp(k):
        kit.wait_on(fresh.at[k, c, z, 1 - xl], state["fx", k])
        ring_b[k].gather(1 - xl)

    def bf(k):
        ring_b[k].forward()
        ring_b[k].await_rest()

    def bc(k):
        ring_b[k].await_far()
        state["fc", k] = kit.recv_slots(1)
        mine = fresh.at[k, c]
        kit.send(mine, mine, other, state["fc", k])

    def merge(k):
        kit.wait_on(fresh.at[k, 1 - c], state["fc", k])
        rows = pl.ds(k * PART, PART)
        for target in range(16):
            cols = pl.ds(target * SHARE, SHARE)
            got = fresh[k, target % 2, target // 4, (target // 2) % 2]
            cd[rows, cols] = (mix_rate * f32(w[rows, cols]) + (1.0 - mix_rate) * f32(got)).astype(
                jnp.bfloat16
            )
        kit.out(cd.at[rows], merged_o.at[rows])

    steps = {
        "mm1": mm1, "xadd": xadd, "mid": mid, "end": end, "norm": norm, "agp": agp, "agf": agf, "agx": agx, "mm2": mm2, "mm3": mm3,
        "gg": gain_sum, "dec": decode, "zs": zs, "zm": zm, "ze": ze, "up": update, "bp": bp, "bf": bf, "bc": bc, "mg": merge,
    }
    for name, number in SCHEDULE:
        steps[name](number)
    for wait in kit.open:
        wait()


def place_kernel(*refs):
    count = (len(refs) - 2) // 3
    got, put, held = refs[:count], refs[count : 2 * count], refs[2 * count : 3 * count]
    come, leave = refs[3 * count :]
    pieces = []
    for i in range(count):
        rows = got[i].shape[0]
        step = PLACE_ROWS if rows % PLACE_ROWS == 0 else rows
        pieces += [(i, pl.ds(at, step)) for at in range(0, rows, step)]
    first = [
        pltpu.make_async_copy(got[i].at[rows], held[i].at[rows], come.at[n])
        for n, (i, rows) in enumerate(pieces)
    ]
    second = [
        pltpu.make_async_copy(held[i].at[rows], put[i].at[rows], leave.at[n])
        for n, (i, rows) in enumerate(pieces)
    ]
    for copy in first:
        copy.start()
    for n, copy in enumerate(second):
        first[n].wait()
        copy.start()
    for copy in second:
        copy.wait()


def shards(hidden, inner_down, residual_in, gain, cotangent, codes, scales, outer_params, momentum):
    anywhere = pl.BlockSpec(memory_space=pl.ANY)
    bf, ft = jnp.bfloat16, jnp.float32
    vmem = pltpu.VMEM
    results = pl.pallas_call(
        sync_kernel,
        out_shape=(
            jax.ShapeDtypeStruct(residual_in.shape, bf),
            jax.ShapeDtypeStruct(hidden.shape, bf),
            jax.ShapeDtypeStruct((1, D), ft),
            jax.ShapeDtypeStruct(outer_params.shape, ft),
            jax.ShapeDtypeStruct(momentum.shape, ft),
            jax.ShapeDtypeStruct(codes.shape[1:], bf),
        ),
        in_specs=[pl.BlockSpec(memory_space=pltpu.HBM)] * 9,
        out_specs=(anywhere,) * 6,
        scratch_shapes=[
            vmem((UNITS, D), bf),
            vmem((512, UNITS), bf),
            vmem((8 * ROWS, UNITS), bf),
            vmem((CHUNKS, 4, 2, ROWS, D), bf),
            vmem((CHUNKS, 2, ROWS, D), bf),
            vmem((CHUNKS, 2, ROWS, D), bf),
            vmem((CHUNKS, 2, ROWS, D), bf),
            vmem((CHUNKS, ROWS, D), bf),
            vmem((4, ROWS, D), bf),
            vmem((CHUNKS, 4, 2, ROWS, D), bf),
            vmem((64, D), bf),
            vmem((64, D), bf),
            vmem((1, D), ft),
            vmem((ROWS, D), ft),
            vmem((64, D), bf),
            vmem((512, UNITS), bf),
            vmem((8, D), ft),
            vmem((4, 1, D), ft),
            vmem((3, 1, D), ft),
            vmem((FRAG_ROWS, D), bf),
            vmem((D // BLOCK, FRAG_ROWS), ft),
            vmem((PARTS, 2, 4, 2, PART, SHARE), bf),
            vmem((PARTS, 4, 2, PART, SHARE), bf),
            vmem((PARTS, 2, PART, SHARE), bf),
            vmem((PARTS, 2, PART, SHARE), bf),
            vmem((PARTS, 2, PART, SHARE), bf),
            vmem((PARTS, PART, SHARE), bf),
            vmem((PARTS, 2, 4, 2, PART, SHARE), bf),
            vmem((FRAG_ROWS, SHARE), ft),
            vmem((FRAG_ROWS, SHARE), ft),
            pltpu.SemaphoreType.DMA((N_SEND,)),
            pltpu.SemaphoreType.DMA((N_RECV,)),
            pltpu.SemaphoreType.DMA((N_LOCAL,)),
        ],
        compiler_params=pltpu.CompilerParams(
            collective_id=0, has_side_effects=True, vmem_limit_bytes=60 * 2**20
        ),
        cost_estimate=pl.CostEstimate(
            flops=4 * 512 * UNITS * D, bytes_accessed=28 * 2**20, transcendentals=0
        ),
        name="sync_step",
    )(
        hidden,
        inner_down[0],
        residual_in,
        gain.reshape(1, D),
        cotangent,
        codes[0],
        scales[0].T,
        outer_params,
        momentum,
    )
    normed, grad_hidden, grad_gain, new_params, new_momentum, merged = pl.pallas_call(
        place_kernel,
        out_shape=tuple(jax.ShapeDtypeStruct(v.shape, v.dtype) for v in results),
        in_specs=[anywhere] * 6,
        out_specs=(anywhere,) * 6,
        scratch_shapes=[pltpu.VMEM(v.shape, v.dtype) for v in results]
        + [pltpu.SemaphoreType.DMA((24,)), pltpu.SemaphoreType.DMA((24,))],
        compiler_params=pltpu.CompilerParams(vmem_limit_bytes=60 * 2**20),
        name="place_results",
    )(*results)
    return (normed, grad_hidden, grad_gain, new_params, new_momentum, merged[None])


def solution(mesh):
    placed = (
        P("replica", "mp"),
        P("replica", "mp", None),
        P(("replica", "mp"), None),
        P(),
        P(("replica", "mp"), None),
        P("replica", "mp", None),
        P("replica", "mp", None),
        P("mp", "replica"),
        P("mp", "replica"),
    )
    return jax.shard_map(
        shards,
        mesh=mesh,
        in_specs=placed,
        out_specs=(
            P(("replica", "mp"), None),
            P("replica", "mp"),
            P("replica", None),
            P("mp", "replica"),
            P("mp", "replica"),
            P("replica", "mp", None),
        ),
        check_vma=False,
    )
```

```python
import functools

import jax
import jax.numpy as jnp
from jax import lax
from jax.experimental import pallas as pl
from jax.experimental.pallas import tpu as pltpu
from jax.sharding import PartitionSpec as P

FF = 7168
BLOCK = 128
MESH = pl.DeviceIdType.MESH

momentum_rate = 0.9
outer_rate = 0.7
mix_rate = 0.5

D = 4096
UNITS = 896
ROWS = 16
CHUNKS = 4
COL_PARTS = (1, 1, 1, 2)
PARTS = 2
FRAG_ROWS = 512
PART = FRAG_ROWS // PARTS
SHARE = 256
HALF = D // 2
X_FIRST = (False, True, False, False)
CUT = 512
N_SEND, N_RECV, N_LOCAL = 160, 160, 40

SCHEDULE = (
    ("mm1", 0), ("mm1", 1), ("dec", 0), ("dec", 1), ("zs", 0), ("mid", 0), ("zs", 1), ("mm1", 2),
    ("mm1", 3), ("zm", 0), ("end", 0), ("mid", 2), ("xadd", 1), ("zm", 1), ("mid", 3), ("norm", 0),
    ("mid", 13), ("ze", 0), ("agp", 0), ("ze", 1), ("end", 2), ("mid", 1), ("up", 0), ("end", 3),
    ("up", 1), ("norm", 2), ("end", 13), ("bp", 0), ("agf", 0), ("end", 1), ("norm", 1), ("bp", 1),
    ("bf", 0), ("agp", 2), ("agx", 0), ("norm", 3), ("gg", 0), ("bf", 1), ("agf", 1), ("mm2", 0),
    ("bc", 0), ("gg", 1), ("agf", 2), ("agp", 3), ("mm3", 0), ("agp", 13), ("bc", 1), ("mg", 0),
    ("gg", 2), ("mg", 1), ("agx", 1), ("agx", 2), ("mm2", 2), ("agf", 3), ("mm3", 2), ("gg", 3),
    ("agf", 13), ("mm2", 1), ("agx", 3), ("mm3", 1), ("agx", 13), ("mm2", 3), ("mm3", 3),
)


class Ring:
    def __init__(self, kit, pos, nxt, prv):
        self.kit, self.pos, self.nxt, self.prv = kit, pos, nxt, prv

    def at(self, step):
        return lax.rem(self.pos + (step % 4), 4)

    def scatter(self, piece, fwd, own, total):
        kit = self.kit
        self.piece, self.fwd, self.own, self.total = piece, fwd, own, total
        two = self.at(2)
        self.got_fwd = (
            kit.send(piece(two, 0), fwd(0), self.nxt),
            kit.send(piece(two, 1), fwd(1), self.prv),
        )
        got_right = kit.send(piece(self.at(1), 1), own(1), self.nxt)
        got_left = kit.send(piece(self.at(3), 0), own(0), self.prv)
        self.got_own = (got_left, got_right)

    def middle(self):
        kit, out = self.kit, []
        for k, (step, to) in enumerate(((1, self.nxt), (3, self.prv))):
            self.got_fwd[k].wait_recv()
            mine = self.piece(self.at(step), k)
            add_into(mine, self.fwd(k))
            out.append(kit.send(mine, self.total(k), to))
        self.got_total = out

    def finish(self):
        for k in range(2):
            self.got_own[k].wait_recv()
            self.got_total[k].wait_recv()

    def gather_open(self, slot):
        self.slot = slot
        self.base = [self.kit.recv_slots(2), self.kit.recv_slots(2)]

    def gather(self, k):
        kit, mine = self.kit, self.slot(self.pos, k)
        kit.send(mine, mine, self.nxt, self.base[0] + k)
        kit.send(mine, mine, self.prv, self.base[1] + k)

    def await_near(self, way, k):
        there = self.slot(self.at(3 if way == 0 else 1), k)
        self.kit.wait_on(there, self.base[way] + k)

    def forward(self):
        kit = self.kit
        self.far = []
        for k, (step, to) in enumerate(((3, self.nxt), (1, self.prv))):
            self.await_near(k, k)
            there = self.slot(self.at(step), k)
            index = kit.recv_slots(1)
            kit.send(there, there, to, index)
            self.far.append(index)

    def await_rest(self):
        self.await_near(0, 1)
        self.await_near(1, 0)

    def await_far(self):
        for k in range(2):
            self.kit.wait_on(self.slot(self.at(2), k), self.far[k])


class Kit:
    def __init__(self, ssem, rsem, lsem):
        self.ssem, self.rsem, self.lsem = ssem, rsem, lsem
        self.sends, self.recvs, self.locals = 0, 0, 0
        self.open = []

    def recv_slots(self, n):
        self.recvs += n
        assert self.recvs <= N_RECV
        return self.recvs - n

    def send(self, src, dst, to, index=None):
        if index is None:
            index = self.recv_slots(1)
        copy = pltpu.make_async_remote_copy(
            src_ref=src,
            dst_ref=dst,
            send_sem=self.ssem.at[self.sends],
            recv_sem=self.rsem.at[index],
            device_id=to,
            device_id_type=MESH,
        )
        self.sends += 1
        assert self.sends <= N_SEND
        copy.start()
        self.open.append(copy.wait_send)
        return copy

    def wait_on(self, ref, index):
        pltpu.make_async_copy(ref, ref, self.rsem.at[index]).wait()

    def local(self, src, dst):
        copy = pltpu.make_async_copy(src, dst, self.lsem.at[self.locals])
        self.locals += 1
        assert self.locals <= N_LOCAL
        copy.start()
        return copy


def f32(value):
    return value.astype(jnp.float32)


def add_into(a, b):
    a[...] = (f32(a[...]) + f32(b[...])).astype(jnp.bfloat16)


def sync_kernel(
    hidden, weights, resid, gain, cot, codes, scales, params, mom,
    nrm, hg, gsum, pr, mo, cd,
    w, hid, lhs, prod, a_fwd, a_own, a_sum, a_x, a_x4, gm, res, ct, gn, mixed, gg, gs, gr,
    sc, dec, core_in, b_fwd, b_own, b_sum, b_x, fresh,
    ssem, rsem, lsem,
):
    kit = Kit(ssem, rsem, lsem)
    r, m = lax.axis_index("replica"), lax.axis_index("mp")
    z, xl, c = r // 4, lax.rem(r // 2, 2), lax.rem(r, 2)
    xh, y = m // 4, lax.rem(m, 4)

    def place(z, xl, c, xh, y):
        return (z * 4 + xl * 2 + c, xh * 4 + y)

    y_next, y_prev = place(z, xl, c, xh, lax.rem(y + 1, 4)), place(z, xl, c, xh, lax.rem(y + 3, 4))
    z_next, z_prev = place(lax.rem(z + 1, 4), xl, c, xh, y), place(lax.rem(z + 3, 4), xl, c, xh, y)
    x_far, x_near, other = place(z, xl, c, 1 - xh, y), place(z, 1 - xl, c, xh, y), place(z, xl, 1 - c, xh, y)

    load_hid = kit.local(hidden, hid)
    width = D // 4
    load_w = [
        kit.local(weights.at[:, pl.ds(i * width, width)], w.at[:, pl.ds(i * width, width)])
        for i in range(4)
    ]
    loads = {}

    def load_rest():
        loads["sc"] = kit.local(scales, sc)
        for i in range(PARTS):
            rows = pl.ds(i * PART, PART)
            loads["cd", i] = kit.local(codes.at[rows], cd.at[rows])
        loads["norm"] = [kit.local(resid, res), kit.local(cot, ct), kit.local(gain, gn)]
        loads["outer"] = [kit.local(params, pr), kit.local(mom, mo)]

    barrier = pltpu.get_barrier_semaphore()
    peers = (y_next, y_prev, z_next, z_prev, x_far, x_near, other)
    for peer in peers:
        pl.semaphore_signal(barrier, inc=1, device_id=peer, device_id_type=MESH)

    scale_ff = FF ** (-0.5)
    ring_a = {}
    ring_b = [Ring(kit, z, z_next, z_prev) for _ in range(PARTS)]
    state = {}
    load_hid.wait()

    def half(k):
        return pl.ds(k * HALF, HALF)

    def part_of(i, p):
        return pl.ds(p * (D // COL_PARTS[i]), D // COL_PARTS[i])

    def ring_start(i):
        if X_FIRST[i]:
            ring_a[i] = Ring(kit, y, y_next, y_prev)
            ring_a[i].scatter(
                lambda pos, k: prod.at[i, pos, xh, :, half(k)],
                lambda k: a_fwd.at[i, 0, :, half(k)],
                lambda k: a_own.at[i, 0, :, half(k)],
                lambda k: a_sum.at[i, 0, :, half(k)],
            )
            return
        for p in range(COL_PARTS[i]):
            cols = part_of(i, p)
            ring_a[i + 10 * p] = Ring(kit, y, y_next, y_prev)
            ring_a[i + 10 * p].scatter(
                lambda pos, k, cols=cols: prod.at[i, pos, k, :, cols],
                lambda k, cols=cols: a_fwd.at[i, k, :, cols],
                lambda k, cols=cols: a_own.at[i, k, :, cols],
                lambda k, cols=cols: a_sum.at[i, k, :, cols],
            )

    def mm1(i):
        for yy in range(4):
            for xx in range(2):
                lhs[pl.ds((yy * 2 + xx) * ROWS, ROWS), :] = hid[
                    pl.ds((xx * 4 + yy) * 64 + i * ROWS, ROWS), :
                ]
        for q in range(4):
            if i == 0:
                load_w[q].wait()
            cols = pl.ds(q * width, width)
            out = jnp.dot(lhs[...], w[:, cols], preferred_element_type=jnp.float32)
            out = (out * scale_ff).astype(jnp.bfloat16)
            prod[i, :, :, :, cols] = out.reshape(4, 2, ROWS, width)
        if i == 0:
            load_rest()
            pl.semaphore_wait(barrier, len(peers))

        if X_FIRST[i]:
            state["x4", i] = kit.send(prod.at[i, :, 1 - xh], a_x4, x_far)
        else:
            ring_start(i)

    def xadd(i):
        if not X_FIRST[i]:
            return
        state["x4", i].wait_recv()
        for pos in range(4):
            add_into(prod.at[i, pos, xh], a_x4.at[pos])
        ring_start(i)

    def mid(i):
        ring_a[i].middle()

    def end(number):
        p, i = divmod(number, 10)
        ring_a[number].finish()
        if X_FIRST[i]:
            return
        k, cols = 1 - xh, part_of(i, p)
        gone = prod.at[i, y, k, :, cols]
        total = f32(gone[...]) + f32(a_own[i, k, :, cols]) + f32(a_sum[i, k, :, cols])
        gone[...] = total.astype(jnp.bfloat16)
        state["x", number] = kit.send(gone, a_x.at[i, :, cols], x_far)

    def norm(i):
        if i == 0:
            for load in loads["norm"]:
                load.wait()
        if not X_FIRST[i]:
            for p in range(COL_PARTS[i]):
                state["x", i + 10 * p].wait_recv()
        rows = pl.ds(i * ROWS, ROWS)
        step = D // 4
        square = jnp.zeros((ROWS, 1), jnp.float32)
        for q in range(4):
            cols = pl.ds(q * step, step)
            if X_FIRST[i]:
                terms = (prod[i, y, xh, :, cols], a_own[i, 0, :, cols], a_sum[i, 0, :, cols])
            else:
                terms = (prod[i, y, xh, :, cols], a_own[i, xh, :, cols], a_sum[i, xh, :, cols], a_x[i, :, cols])
            value = f32(res[rows, cols])
            for term in terms:
                value = value + f32(term)
            mixed[:, cols] = value
            square = square + jnp.sum(value * value, -1, keepdims=True)
        inv = lax.rsqrt(square / D + 1e-05)
        along = jnp.zeros((ROWS, 1), jnp.float32)
        for q in range(4):
            cols = pl.ds(q * step, step)
            unit = mixed[:, cols] * inv
            mixed[:, cols] = unit
            gain_row = gn[:, cols]
            nrm[rows, cols] = (unit * gain_row).astype(jnp.bfloat16)
            cot_rows = f32(ct[rows, cols])
            along = along + jnp.sum(cot_rows * gain_row * unit, -1, keepdims=True)
            pair = cot_rows * unit
            pair = pair[:8] + pair[8:]
            if i == 0:
                gg[:, cols] = pair
            else:
                gg[:, cols] += pair
        along = along / D
        for q in range(4):
            cols = pl.ds(q * step, step)
            scaled = f32(ct[rows, cols]) * gn[:, cols]
            gm[i, y, xh, :, cols] = (inv * (scaled - mixed[:, cols] * along)).astype(jnp.bfloat16)
        if X_FIRST[i]:
            ring_a[i].gather_open(lambda pos, k: gm.at[i, pos, xh, :, half(k)])
            ring_a[i].gather(0)
            ring_a[i].gather(1)
            state["gx", i] = kit.recv_slots(4)
            mine = gm.at[i, y, xh]
            kit.send(mine, mine, x_far, state["gx", i] + y)
        else:
            for p in range(COL_PARTS[i]):
                number, cols = i + 10 * p, part_of(i, p)
                ring_a[number].gather_open(lambda pos, k, cols=cols: gm.at[i, pos, k, :, cols])
                mine = gm.at[i, y, xh, :, cols]
                state["gx", number] = kit.recv_slots(1)
                kit.send(mine, mine, x_far, state["gx", number])
                ring_a[number].gather(xh)

    def agp(number):
        p, i = divmod(number, 10)
        if not X_FIRST[i]:
            kit.wait_on(gm.at[i, y, 1 - xh, :, part_of(i, p)], state["gx", number])
            ring_a[number].gather(1 - xh)

    def agf(number):
        p, i = divmod(number, 10)
        ring = ring_a[number]
        ring.forward()
        if X_FIRST[i]:
            ring.await_rest()
            for step in (1, 3):
                there = gm.at[i, ring.at(step), xh]
                kit.send(there, there, x_far, state["gx", i] + ring.at(step))

    def agx(number):
        p, i = divmod(number, 10)
        ring = ring_a[number]
        ring.await_far()
        if X_FIRST[i]:
            there = gm.at[i, ring.at(2), xh]
            kit.send(there, there, x_far, state["gx", i] + ring.at(2))
        else:
            ring.await_rest()

    def back(i, first, count):
        units = pl.ds(first, count)
        out = lax.dot_general(
            w[units, :],
            gm[i].reshape(8 * ROWS, D),
            (((1,), (1,)), ((), ())),
            preferred_element_type=jnp.float32,
        )
        out = (out * scale_ff).T.astype(jnp.bfloat16)
        for yy in range(4):
            for xx in range(2):
                at = (yy * 2 + xx) * ROWS
                hg[pl.ds((xx * 4 + yy) * 64 + i * ROWS, ROWS), units] = out[at : at + ROWS]

    def mm2(i):
        if X_FIRST[i]:
            for pos in range(4):
                kit.wait_on(gm.at[i, pos, 1 - xh], state["gx", i] + pos)
        back(i, 0, CUT)

    def mm3(i):
        back(i, CUT, UNITS - CUT)

    def gain_sum(step):
        partner = (x_far, None, None)[step] if step < 1 else None
        if step == 0:
            gs[0] = jnp.sum(gg[...], 0, keepdims=True)
        elif step < 4:
            state["gg", step - 1].wait_recv()
            gs[step] = gs[step - 1] + gr[step - 1]
        if step == 1:
            partner = place(z, xl, c, xh, y + 1 - 2 * lax.rem(y, 2))
        if step == 2:
            partner = place(z, xl, c, xh, 3 - y)
        if step < 3:
            state["gg", step] = kit.send(gs.at[step], gr.at[step], partner)
        else:
            gsum[...] = gs[3]

    def decode(k):
        if k == 0:
            loads["sc"].wait()
        loads["cd", k].wait()
        rows = pl.ds(k * PART, PART)
        factors = sc[:, rows].T
        for j in range(D // BLOCK):
            target, part = j // 2, j % 2
            value = f32(cd[rows, pl.ds(j * BLOCK, BLOCK)]) * factors[:, j : j + 1]
            dec[k, target % 2, target // 4, (target // 2) % 2, :, pl.ds(part * BLOCK, BLOCK)] = value.astype(
                jnp.bfloat16
            )
        state["core", k] = kit.send(dec.at[k, 1 - c], core_in.at[k], other)

    def zs(k):
        state["core", k].wait_recv()
        for step in (2, 1, 3, 0):
            at = ring_b[k].at(step)
            for way in range(2):
                add_into(dec.at[k, c, at, way], core_in.at[k, at, way])
        ring_b[k].scatter(
            lambda pos, way: dec.at[k, c, pos, way],
            lambda way: b_fwd.at[k, way],
            lambda way: b_own.at[k, way],
            lambda way: b_sum.at[k, way],
        )

    def zm(k):
        ring_b[k].middle()

    def ze(k):
        ring_b[k].finish()
        way = 1 - xl
        gone = dec.at[k, c, z, way]
        gone[...] = (f32(gone[...]) + f32(b_own[k, way]) + f32(b_sum[k, way])).astype(jnp.bfloat16)
        state["xl", k] = kit.send(gone, b_x.at[k], x_near)

    def update(k):
        if k == 0:
            for load in loads["outer"]:
                load.wait()
        state["xl", k].wait_recv()
        rows = pl.ds(k * PART, PART)
        total = f32(dec[k, c, z, xl]) + f32(b_own[k, xl]) + f32(b_sum[k, xl]) + f32(b_x[k])
        step = total / 16
        new_mom = momentum_rate * mo[rows, :] + step
        new_params = pr[rows, :] - outer_rate * (step + momentum_rate * new_mom)
        mo[rows, :] = new_mom
        pr[rows, :] = new_params
        mine = fresh.at[k, c, z, xl]
        mine[...] = new_params.astype(jnp.bfloat16)
        ring_b[k].gather_open(lambda pos, way: fresh.at[k, c, pos, way])
        state["fx", k] = kit.recv_slots(1)
        kit.send(mine, mine, x_near, state["fx", k])
        ring_b[k].gather(xl)

    def bp(k):
        kit.wait_on(fresh.at[k, c, z, 1 - xl], state["fx", k])
        ring_b[k].gather(1 - xl)

    def bf(k):
        ring_b[k].forward()
        ring_b[k].await_rest()

    def bc(k):
        ring_b[k].await_far()
        state["fc", k] = kit.recv_slots(1)
        mine = fresh.at[k, c]
        kit.send(mine, mine, other, state["fc", k])

    def merge(k):
        kit.wait_on(fresh.at[k, 1 - c], state["fc", k])
        rows = pl.ds(k * PART, PART)
        for target in range(16):
            cols = pl.ds(target * SHARE, SHARE)
            got = fresh[k, target % 2, target // 4, (target // 2) % 2]
            cd[rows, cols] = (mix_rate * f32(w[rows, cols]) + (1.0 - mix_rate) * f32(got)).astype(
                jnp.bfloat16
            )

    steps = {
        "mm1": mm1, "xadd": xadd, "mid": mid, "end": end, "norm": norm, "agp": agp, "agf": agf, "agx": agx, "mm2": mm2, "mm3": mm3,
        "gg": gain_sum, "dec": decode, "zs": zs, "zm": zm, "ze": ze, "up": update, "bp": bp, "bf": bf, "bc": bc, "mg": merge,
    }
    for name, number in SCHEDULE:
        steps[name](number)
    for wait in kit.open:
        wait()


def place_kernel(*refs):
    sems = refs[-1]
    count = (len(refs) - 1) // 2
    copies = [pltpu.make_async_copy(refs[i], refs[count + i], sems.at[i]) for i in range(count)]
    for copy in copies:
        copy.start()
    for copy in copies:
        copy.wait()


def shards(hidden, inner_down, residual_in, gain, cotangent, codes, scales, outer_params, momentum):
    anywhere = pl.BlockSpec(memory_space=pl.ANY)
    bf, ft = jnp.bfloat16, jnp.float32
    vmem = pltpu.VMEM
    results = pl.pallas_call(
        sync_kernel,
        out_shape=(
            vmem(residual_in.shape, bf),
            vmem(hidden.shape, bf),
            vmem((1, D), ft),
            vmem(outer_params.shape, ft),
            vmem(momentum.shape, ft),
            vmem(codes.shape[1:], bf),
        ),
        in_specs=[pl.BlockSpec(memory_space=pltpu.HBM)] * 9,
        out_specs=(pl.BlockSpec(memory_space=pltpu.VMEM),) * 6,
        scratch_shapes=[
            vmem((UNITS, D), bf),
            vmem((512, UNITS), bf),
            vmem((8 * ROWS, UNITS), bf),
            vmem((CHUNKS, 4, 2, ROWS, D), bf),
            vmem((CHUNKS, 2, ROWS, D), bf),
            vmem((CHUNKS, 2, ROWS, D), bf),
            vmem((CHUNKS, 2, ROWS, D), bf),
            vmem((CHUNKS, ROWS, D), bf),
            vmem((4, ROWS, D), bf),
            vmem((CHUNKS, 4, 2, ROWS, D), bf),
            vmem((64, D), bf),
            vmem((64, D), bf),
            vmem((1, D), ft),
            vmem((ROWS, D), ft),
            vmem((8, D), ft),
            vmem((4, 1, D), ft),
            vmem((3, 1, D), ft),
            vmem((D // BLOCK, FRAG_ROWS), ft),
            vmem((PARTS, 2, 4, 2, PART, SHARE), bf),
            vmem((PARTS, 4, 2, PART, SHARE), bf),
            vmem((PARTS, 2, PART, SHARE), bf),
            vmem((PARTS, 2, PART, SHARE), bf),
            vmem((PARTS, 2, PART, SHARE), bf),
            vmem((PARTS, PART, SHARE), bf),
            vmem((PARTS, 2, 4, 2, PART, SHARE), bf),
            pltpu.SemaphoreType.DMA((N_SEND,)),
            pltpu.SemaphoreType.DMA((N_RECV,)),
            pltpu.SemaphoreType.DMA((N_LOCAL,)),
        ],
        compiler_params=pltpu.CompilerParams(
            collective_id=0, has_side_effects=True, vmem_limit_bytes=56 * 2**20
        ),
        cost_estimate=pl.CostEstimate(
            flops=4 * 512 * UNITS * D, bytes_accessed=28 * 2**20, transcendentals=0
        ),
        name="sync_step",
    )(
        hidden,
        inner_down[0],
        residual_in,
        gain.reshape(1, D),
        cotangent,
        codes[0],
        scales[0].T,
        outer_params,
        momentum,
    )
    normed, grad_hidden, grad_gain, new_params, new_momentum, merged = pl.pallas_call(
        place_kernel,
        out_shape=tuple(jax.ShapeDtypeStruct(v.shape, v.dtype) for v in results),
        in_specs=[pl.BlockSpec(memory_space=pltpu.VMEM)] * 6,
        out_specs=(anywhere,) * 6,
        scratch_shapes=[pltpu.SemaphoreType.DMA((6,))],
        compiler_params=pltpu.CompilerParams(vmem_limit_bytes=2**20),
        name="place_results",
    )(*results)
    return (normed, grad_hidden, grad_gain, new_params, new_momentum, merged[None])


def solution(mesh):
    placed = (
        P("replica", "mp"),
        P("replica", "mp", None),
        P(("replica", "mp"), None),
        P(),
        P(("replica", "mp"), None),
        P("replica", "mp", None),
        P("replica", "mp", None),
        P("mp", "replica"),
        P("mp", "replica"),
    )
    return jax.shard_map(
        shards,
        mesh=mesh,
        in_specs=placed,
        out_specs=(
            P(("replica", "mp"), None),
            P("replica", "mp"),
            P("replica", None),
            P("mp", "replica"),
            P("mp", "replica"),
            P("replica", "mp", None),
        ),
        check_vma=False,
    )
```

```python
import functools

import jax
import jax.numpy as jnp
from jax import lax
from jax.experimental import pallas as pl
from jax.experimental.pallas import tpu as pltpu
from jax.sharding import PartitionSpec as P

FF = 7168
BLOCK = 128
MESH = pl.DeviceIdType.MESH

momentum_rate = 0.9
outer_rate = 0.7
mix_rate = 0.5

D = 4096
UNITS = 896
ROWS = 16
CHUNKS = 4
COL_PARTS = (2, 1, 2, 2)
PARTS = 2
FRAG_ROWS = 512
PART = FRAG_ROWS // PARTS
SHARE = 256
HALF = D // 2
X_FIRST = (False, True, False, False)
CUT = 512
N_SEND, N_RECV, N_LOCAL = 160, 160, 40

SCHEDULE = (
    ("mm1", 0), ("mm1", 1), ("dec", 1), ("mid", 0), ("zs", 1), ("mid", 10), ("dec", 0), ("mm1", 2),
    ("end", 0), ("zs", 0), ("end", 10), ("zm", 1), ("mid", 2), ("mm1", 3), ("mid", 12), ("xadd", 1),
    ("zm", 0), ("end", 2), ("norm", 0), ("mid", 3), ("mid", 13), ("ze", 1), ("agp", 0), ("end", 12),
    ("ze", 0), ("agp", 10), ("mid", 1), ("up", 1), ("norm", 2), ("end", 3), ("up", 0), ("end", 13),
    ("agf", 0), ("bp", 1), ("agf", 10), ("agp", 2), ("end", 1), ("norm", 1), ("agp", 12), ("agx", 0),
    ("bp", 0), ("agx", 10), ("norm", 3), ("gg", 0), ("mm2", 0), ("bf", 1), ("mm3", 0), ("agf", 2),
    ("agf", 1), ("gg", 1), ("bf", 0), ("agf", 12), ("agp", 3), ("agp", 13), ("bc", 1), ("agx", 2),
    ("mm2", 2), ("gg", 2), ("agx", 1), ("mg", 1), ("bc", 0), ("agx", 12), ("mm3", 2), ("agf", 3),
    ("gg", 3), ("mg", 0), ("agf", 13), ("mm2", 1), ("agx", 3), ("mm2", 3), ("agx", 13), ("mm3", 3),
    ("mm3", 1),
)


class Ring:
    def __init__(self, kit, pos, nxt, prv):
        self.kit, self.pos, self.nxt, self.prv = kit, pos, nxt, prv

    def at(self, step):
        return lax.rem(self.pos + (step % 4), 4)

    def scatter(self, piece, fwd, own, total):
        kit = self.kit
        self.piece, self.fwd, self.own, self.total = piece, fwd, own, total
        two = self.at(2)
        self.got_fwd = (
            kit.send(piece(two, 0), fwd(0), self.nxt),
            kit.send(piece(two, 1), fwd(1), self.prv),
        )
        got_right = kit.send(piece(self.at(1), 1), own(1), self.nxt)
        got_left = kit.send(piece(self.at(3), 0), own(0), self.prv)
        self.got_own = (got_left, got_right)

    def middle(self):
        kit, out = self.kit, []
        for k, (step, to) in enumerate(((1, self.nxt), (3, self.prv))):
            self.got_fwd[k].wait_recv()
            mine = self.piece(self.at(step), k)
            add_into(mine, self.fwd(k))
            out.append(kit.send(mine, self.total(k), to))
        self.got_total = out

    def finish(self):
        for k in range(2):
            self.got_own[k].wait_recv()
            self.got_total[k].wait_recv()

    def gather_open(self, slot):
        self.slot = slot
        self.base = [self.kit.recv_slots(2), self.kit.recv_slots(2)]

    def gather(self, k):
        kit, mine = self.kit, self.slot(self.pos, k)
        kit.send(mine, mine, self.nxt, self.base[0] + k)
        kit.send(mine, mine, self.prv, self.base[1] + k)

    def await_near(self, way, k):
        there = self.slot(self.at(3 if way == 0 else 1), k)
        self.kit.wait_on(there, self.base[way] + k)

    def forward(self):
        kit = self.kit
        self.far = []
        for k, (step, to) in enumerate(((3, self.nxt), (1, self.prv))):
            self.await_near(k, k)
            there = self.slot(self.at(step), k)
            index = kit.recv_slots(1)
            kit.send(there, there, to, index)
            self.far.append(index)

    def await_rest(self):
        self.await_near(0, 1)
        self.await_near(1, 0)

    def await_far(self):
        for k in range(2):
            self.kit.wait_on(self.slot(self.at(2), k), self.far[k])


class Kit:
    def __init__(self, ssem, rsem, lsem):
        self.ssem, self.rsem, self.lsem = ssem, rsem, lsem
        self.sends, self.recvs, self.locals = 0, 0, 0
        self.open = []

    def recv_slots(self, n):
        self.recvs += n
        assert self.recvs <= N_RECV
        return self.recvs - n

    def send(self, src, dst, to, index=None):
        if index is None:
            index = self.recv_slots(1)
        copy = pltpu.make_async_remote_copy(
            src_ref=src,
            dst_ref=dst,
            send_sem=self.ssem.at[self.sends],
            recv_sem=self.rsem.at[index],
            device_id=to,
            device_id_type=MESH,
        )
        self.sends += 1
        assert self.sends <= N_SEND
        copy.start()
        self.open.append(copy.wait_send)
        return copy

    def wait_on(self, ref, index):
        pltpu.make_async_copy(ref, ref, self.rsem.at[index]).wait()

    def local(self, src, dst):
        copy = pltpu.make_async_copy(src, dst, self.lsem.at[self.locals])
        self.locals += 1
        assert self.locals <= N_LOCAL
        copy.start()
        return copy


def f32(value):
    return value.astype(jnp.float32)


def add_into(a, b):
    a[...] = (f32(a[...]) + f32(b[...])).astype(jnp.bfloat16)


def sync_kernel(
    hidden, weights, resid, gain, cot, codes, scales, params, mom,
    nrm, hg, gsum, pr, mo, cd,
    w, hid, lhs, prod, a_fwd, a_own, a_sum, a_x, a_x4, gm, res, ct, gn, mixed, acc, gg, gs, gr,
    sc, dec, core_in, b_fwd, b_own, b_sum, b_x, fresh,
    ssem, rsem, lsem,
):
    kit = Kit(ssem, rsem, lsem)
    r, m = lax.axis_index("replica"), lax.axis_index("mp")
    z, xl, c = r // 4, lax.rem(r // 2, 2), lax.rem(r, 2)
    xh, y = m // 4, lax.rem(m, 4)

    def place(z, xl, c, xh, y):
        return (z * 4 + xl * 2 + c, xh * 4 + y)

    y_next, y_prev = place(z, xl, c, xh, lax.rem(y + 1, 4)), place(z, xl, c, xh, lax.rem(y + 3, 4))
    z_next, z_prev = place(lax.rem(z + 1, 4), xl, c, xh, y), place(lax.rem(z + 3, 4), xl, c, xh, y)
    x_far, x_near, other = place(z, xl, c, 1 - xh, y), place(z, 1 - xl, c, xh, y), place(z, xl, 1 - c, xh, y)

    load_hid = kit.local(hidden, hid)
    width = D // 4
    load_w = [
        kit.local(weights.at[:, pl.ds(i * width, width)], w.at[:, pl.ds(i * width, width)])
        for i in range(4)
    ]
    loads = {}

    def load_rest():
        loads["sc"] = kit.local(scales, sc)
        for i in range(PARTS):
            rows = pl.ds(i * PART, PART)
            loads["cd", i] = kit.local(codes.at[rows], cd.at[rows])
        loads["norm"] = [kit.local(resid, res), kit.local(cot, ct), kit.local(gain, gn)]
        loads["outer"] = [kit.local(params, pr), kit.local(mom, mo)]

    barrier = pltpu.get_barrier_semaphore()
    peers = (y_next, y_prev, z_next, z_prev, x_far, x_near, other)
    for peer in peers:
        pl.semaphore_signal(barrier, inc=1, device_id=peer, device_id_type=MESH)

    scale_ff = FF ** (-0.5)
    ring_a = {}
    ring_b = [Ring(kit, z, z_next, z_prev) for _ in range(PARTS)]
    state = {}
    load_hid.wait()

    def half(k):
        return pl.ds(k * HALF, HALF)

    def part_of(i, p):
        return pl.ds(p * (D // COL_PARTS[i]), D // COL_PARTS[i])

    def ring_start(i, p=0):
        if X_FIRST[i]:
            ring_a[i] = Ring(kit, y, y_next, y_prev)
            ring_a[i].scatter(
                lambda pos, k: prod.at[i, pos, xh, :, half(k)],
                lambda k: a_fwd.at[i, 0, :, half(k)],
                lambda k: a_own.at[i, 0, :, half(k)],
                lambda k: a_sum.at[i, 0, :, half(k)],
            )
            return
        cols = part_of(i, p)
        ring_a[i + 10 * p] = Ring(kit, y, y_next, y_prev)
        ring_a[i + 10 * p].scatter(
            lambda pos, k: prod.at[i, pos, k, :, cols],
            lambda k: a_fwd.at[i, k, :, cols],
            lambda k: a_own.at[i, k, :, cols],
            lambda k: a_sum.at[i, k, :, cols],
        )

    def mm1(i):
        for yy in range(4):
            for xx in range(2):
                lhs[pl.ds((yy * 2 + xx) * ROWS, ROWS), :] = hid[
                    pl.ds((xx * 4 + yy) * 64 + i * ROWS, ROWS), :
                ]
        for q in range(4):
            if i == 0:
                load_w[q].wait()
            cols = pl.ds(q * width, width)
            out = jnp.dot(lhs[...], w[:, cols], preferred_element_type=jnp.float32)
            out = (out * scale_ff).astype(jnp.bfloat16)
            prod[i, :, :, :, cols] = out.reshape(4, 2, ROWS, width)
            if i == 0 and q == 4 // COL_PARTS[i] - 1:
                pl.semaphore_wait(barrier, len(peers))
            if not X_FIRST[i] and (q + 1) * COL_PARTS[i] % 4 == 0:
                ring_start(i, (q + 1) * COL_PARTS[i] // 4 - 1)
        if i == 0:
            load_rest()
        if X_FIRST[i]:
            state["x4", i] = kit.send(prod.at[i, :, 1 - xh], a_x4, x_far)

    def xadd(i):
        if not X_FIRST[i]:
            return
        state["x4", i].wait_recv()
        for pos in range(4):
            add_into(prod.at[i, pos, xh], a_x4.at[pos])
        ring_start(i)

    def mid(i):
        ring_a[i].middle()

    def end(number):
        p, i = divmod(number, 10)
        ring_a[number].finish()
        if X_FIRST[i]:
            return
        k, cols = 1 - xh, part_of(i, p)
        gone = prod.at[i, y, k, :, cols]
        total = f32(gone[...]) + f32(a_own[i, k, :, cols]) + f32(a_sum[i, k, :, cols])
        gone[...] = total.astype(jnp.bfloat16)
        state["x", number] = kit.send(gone, a_x.at[i, :, cols], x_far)

    def norm(i):
        for load in loads.pop("norm", ()):
            load.wait()
        if not X_FIRST[i]:
            for p in range(COL_PARTS[i]):
                state["x", i + 10 * p].wait_recv()
        rows = pl.ds(i * ROWS, ROWS)
        step = D // 4
        square = jnp.zeros((ROWS, 1), jnp.float32)
        for q in range(4):
            cols = pl.ds(q * step, step)
            if X_FIRST[i]:
                terms = (prod[i, y, xh, :, cols], a_own[i, 0, :, cols], a_sum[i, 0, :, cols])
            else:
                terms = (prod[i, y, xh, :, cols], a_own[i, xh, :, cols], a_sum[i, xh, :, cols], a_x[i, :, cols])
            value = f32(res[rows, cols])
            for term in terms:
                value = value + f32(term)
            mixed[:, cols] = value
            square = square + jnp.sum(value * value, -1, keepdims=True)
        inv = lax.rsqrt(square / D + 1e-05)
        along = jnp.zeros((ROWS, 1), jnp.float32)
        for q in range(4):
            cols = pl.ds(q * step, step)
            unit = mixed[:, cols] * inv
            mixed[:, cols] = unit
            gain_row = gn[:, cols]
            nrm[rows, cols] = (unit * gain_row).astype(jnp.bfloat16)
            cot_rows = f32(ct[rows, cols])
            along = along + jnp.sum(cot_rows * gain_row * unit, -1, keepdims=True)
            pair = cot_rows * unit
            pair = pair[:8] + pair[8:]
            if i == 0:
                gg[:, cols] = pair
            else:
                gg[:, cols] += pair
        along = along / D
        for q in range(4):
            cols = pl.ds(q * step, step)
            scaled = f32(ct[rows, cols]) * gn[:, cols]
            gm[i, y, xh, :, cols] = (inv * (scaled - mixed[:, cols] * along)).astype(jnp.bfloat16)
        if X_FIRST[i]:
            ring_a[i].gather_open(lambda pos, k: gm.at[i, pos, xh, :, half(k)])
            ring_a[i].gather(0)
            ring_a[i].gather(1)
            state["gx", i] = kit.recv_slots(4)
            mine = gm.at[i, y, xh]
            kit.send(mine, mine, x_far, state["gx", i] + y)
        else:
            for p in range(COL_PARTS[i]):
                number, cols = i + 10 * p, part_of(i, p)
                ring_a[number].gather_open(lambda pos, k, cols=cols: gm.at[i, pos, k, :, cols])
                mine = gm.at[i, y, xh, :, cols]
                state["gx", number] = kit.recv_slots(1)
                kit.send(mine, mine, x_far, state["gx", number])
                ring_a[number].gather(xh)

    def agp(number):
        p, i = divmod(number, 10)
        if not X_FIRST[i]:
            kit.wait_on(gm.at[i, y, 1 - xh, :, part_of(i, p)], state["gx", number])
            ring_a[number].gather(1 - xh)

    def agf(number):
        p, i = divmod(number, 10)
        ring = ring_a[number]
        ring.forward()
        if X_FIRST[i]:
            ring.await_rest()
            for step in (1, 3):
                there = gm.at[i, ring.at(step), xh]
                kit.send(there, there, x_far, state["gx", i] + ring.at(step))

    def agx(number):
        p, i = divmod(number, 10)
        ring = ring_a[number]
        ring.await_far()
        if X_FIRST[i]:
            there = gm.at[i, ring.at(2), xh]
            kit.send(there, there, x_far, state["gx", i] + ring.at(2))
        else:
            ring.await_rest()

    def back(i, units, cols):
        return lax.dot_general(
            w[units, cols],
            gm[i, :, :, :, cols].reshape(8 * ROWS, cols.size),
            (((1,), (1,)), ((), ())),
            preferred_element_type=jnp.float32,
        )

    def back_out(i, units, out):
        out = (out * scale_ff).T.astype(jnp.bfloat16)
        for yy in range(4):
            for xx in range(2):
                at = (yy * 2 + xx) * ROWS
                hg[pl.ds((xx * 4 + yy) * 64 + i * ROWS, ROWS), units] = out[at : at + ROWS]

    def mm2(i):
        if X_FIRST[i]:
            for pos in range(4):
                kit.wait_on(gm.at[i, pos, 1 - xh], state["gx", i] + pos)
        if COL_PARTS[i] == 2:
            acc[i] = back(i, pl.ds(0, UNITS), half(0))
        else:
            units = pl.ds(0, CUT)
            back_out(i, units, back(i, units, pl.ds(0, D)))

    def mm3(i):
        if COL_PARTS[i] == 2:
            units = pl.ds(0, UNITS)
            back_out(i, units, acc[i] + back(i, units, half(1)))
        else:
            units = pl.ds(CUT, UNITS - CUT)
            back_out(i, units, back(i, units, pl.ds(0, D)))

    def gain_sum(step):
        partner = (x_far, None, None)[step] if step < 1 else None
        if step == 0:
            gs[0] = jnp.sum(gg[...], 0, keepdims=True)
        elif step < 4:
            state["gg", step - 1].wait_recv()
            gs[step] = gs[step - 1] + gr[step - 1]
        if step == 1:
            partner = place(z, xl, c, xh, y + 1 - 2 * lax.rem(y, 2))
        if step == 2:
            partner = place(z, xl, c, xh, 3 - y)
        if step < 3:
            state["gg", step] = kit.send(gs.at[step], gr.at[step], partner)
        else:
            gsum[...] = gs[3]

    def decode(k):
        if "sc" in loads:
            loads.pop("sc").wait()
        loads["cd", k].wait()
        rows = pl.ds(k * PART, PART)
        factors = sc[:, rows].T
        for j in range(D // BLOCK):
            target, part = j // 2, j % 2
            value = f32(cd[rows, pl.ds(j * BLOCK, BLOCK)]) * factors[:, j : j + 1]
            dec[k, target % 2, target // 4, (target // 2) % 2, :, pl.ds(part * BLOCK, BLOCK)] = value.astype(
                jnp.bfloat16
            )
        state["core", k] = kit.send(dec.at[k, 1 - c], core_in.at[k], other)

    def zs(k):
        state["core", k].wait_recv()
        for step in (2, 1, 3, 0):
            at = ring_b[k].at(step)
            for way in range(2):
                add_into(dec.at[k, c, at, way], core_in.at[k, at, way])
        ring_b[k].scatter(
            lambda pos, way: dec.at[k, c, pos, way],
            lambda way: b_fwd.at[k, way],
            lambda way: b_own.at[k, way],
            lambda way: b_sum.at[k, way],
        )

    def zm(k):
        ring_b[k].middle()

    def ze(k):
        ring_b[k].finish()
        way = 1 - xl
        gone = dec.at[k, c, z, way]
        gone[...] = (f32(gone[...]) + f32(b_own[k, way]) + f32(b_sum[k, way])).astype(jnp.bfloat16)
        state["xl", k] = kit.send(gone, b_x.at[k], x_near)

    def update(k):
        for load in loads.pop("outer", ()):
            load.wait()
        state["xl", k].wait_recv()
        rows = pl.ds(k * PART, PART)
        total = f32(dec[k, c, z, xl]) + f32(b_own[k, xl]) + f32(b_sum[k, xl]) + f32(b_x[k])
        step = total / 16
        new_mom = momentum_rate * mo[rows, :] + step
        new_params = pr[rows, :] - outer_rate * (step + momentum_rate * new_mom)
        mo[rows, :] = new_mom
        pr[rows, :] = new_params
        mine = fresh.at[k, c, z, xl]
        mine[...] = new_params.astype(jnp.bfloat16)
        ring_b[k].gather_open(lambda pos, way: fresh.at[k, c, pos, way])
        state["fx", k] = kit.recv_slots(1)
        kit.send(mine, mine, x_near, state["fx", k])
        ring_b[k].gather(xl)

    def bp(k):
        kit.wait_on(fresh.at[k, c, z, 1 - xl], state["fx", k])
        ring_b[k].gather(1 - xl)

    def bf(k):
        ring_b[k].forward()
        ring_b[k].await_rest()

    def bc(k):
        ring_b[k].await_far()
        state["fc", k] = kit.recv_slots(1)
        mine = fresh.at[k, c]
        kit.send(mine, mine, other, state["fc", k])

    def merge(k):
        kit.wait_on(fresh.at[k, 1 - c], state["fc", k])
        rows = pl.ds(k * PART, PART)
        for target in range(16):
            cols = pl.ds(target * SHARE, SHARE)
            got = fresh[k, target % 2, target // 4, (target // 2) % 2]
            cd[rows, cols] = (mix_rate * f32(w[rows, cols]) + (1.0 - mix_rate) * f32(got)).astype(
                jnp.bfloat16
            )

    steps = {
        "mm1": mm1, "xadd": xadd, "mid": mid, "end": end, "norm": norm, "agp": agp, "agf": agf, "agx": agx, "mm2": mm2, "mm3": mm3,
        "gg": gain_sum, "dec": decode, "zs": zs, "zm": zm, "ze": ze, "up": update, "bp": bp, "bf": bf, "bc": bc, "mg": merge,
    }
    for name, number in SCHEDULE:
        steps[name](number)
    for wait in kit.open:
        wait()


def place_kernel(*refs):
    sems = refs[-1]
    count = (len(refs) - 1) // 2
    copies = [pltpu.make_async_copy(refs[i], refs[count + i], sems.at[i]) for i in range(count)]
    for copy in copies:
        copy.start()
    for copy in copies:
        copy.wait()


def shards(hidden, inner_down, residual_in, gain, cotangent, codes, scales, outer_params, momentum):
    anywhere = pl.BlockSpec(memory_space=pl.ANY)
    bf, ft = jnp.bfloat16, jnp.float32
    vmem = pltpu.VMEM
    results = pl.pallas_call(
        sync_kernel,
        out_shape=(
            vmem(residual_in.shape, bf),
            vmem(hidden.shape, bf),
            vmem((1, D), ft),
            vmem(outer_params.shape, ft),
            vmem(momentum.shape, ft),
            vmem(codes.shape[1:], bf),
        ),
        in_specs=[pl.BlockSpec(memory_space=pltpu.HBM)] * 9,
        out_specs=(pl.BlockSpec(memory_space=pltpu.VMEM),) * 6,
        scratch_shapes=[
            vmem((UNITS, D), bf),
            vmem((512, UNITS), bf),
            vmem((8 * ROWS, UNITS), bf),
            vmem((CHUNKS, 4, 2, ROWS, D), bf),
            vmem((CHUNKS, 2, ROWS, D), bf),
            vmem((CHUNKS, 2, ROWS, D), bf),
            vmem((CHUNKS, 2, ROWS, D), bf),
            vmem((CHUNKS, ROWS, D), bf),
            vmem((4, ROWS, D), bf),
            vmem((CHUNKS, 4, 2, ROWS, D), bf),
            vmem((64, D), bf),
            vmem((64, D), bf),
            vmem((1, D), ft),
            vmem((ROWS, D), ft),
            vmem((CHUNKS, UNITS, 8 * ROWS), ft),
            vmem((8, D), ft),
            vmem((4, 1, D), ft),
            vmem((3, 1, D), ft),
            vmem((D // BLOCK, FRAG_ROWS), ft),
            vmem((PARTS, 2, 4, 2, PART, SHARE), bf),
            vmem((PARTS, 4, 2, PART, SHARE), bf),
            vmem((PARTS, 2, PART, SHARE), bf),
            vmem((PARTS, 2, PART, SHARE), bf),
            vmem((PARTS, 2, PART, SHARE), bf),
            vmem((PARTS, PART, SHARE), bf),
            vmem((PARTS, 2, 4, 2, PART, SHARE), bf),
            pltpu.SemaphoreType.DMA((N_SEND,)),
            pltpu.SemaphoreType.DMA((N_RECV,)),
            pltpu.SemaphoreType.DMA((N_LOCAL,)),
        ],
        compiler_params=pltpu.CompilerParams(
            collective_id=0, has_side_effects=True, vmem_limit_bytes=56 * 2**20
        ),
        cost_estimate=pl.CostEstimate(
            flops=4 * 512 * UNITS * D, bytes_accessed=28 * 2**20, transcendentals=0
        ),
        name="sync_step",
    )(
        hidden,
        inner_down[0],
        residual_in,
        gain.reshape(1, D),
        cotangent,
        codes[0],
        scales[0].T,
        outer_params,
        momentum,
    )
    normed, grad_hidden, grad_gain, new_params, new_momentum, merged = pl.pallas_call(
        place_kernel,
        out_shape=tuple(jax.ShapeDtypeStruct(v.shape, v.dtype) for v in results),
        in_specs=[pl.BlockSpec(memory_space=pltpu.VMEM)] * 6,
        out_specs=(anywhere,) * 6,
        scratch_shapes=[pltpu.SemaphoreType.DMA((6,))],
        compiler_params=pltpu.CompilerParams(vmem_limit_bytes=2**20),
        name="place_results",
    )(*results)
    return (normed, grad_hidden, grad_gain, new_params, new_momentum, merged[None])


def solution(mesh):
    placed = (
        P("replica", "mp"),
        P("replica", "mp", None),
        P(("replica", "mp"), None),
        P(),
        P(("replica", "mp"), None),
        P("replica", "mp", None),
        P("replica", "mp", None),
        P("mp", "replica"),
        P("mp", "replica"),
    )
    return jax.shard_map(
        shards,
        mesh=mesh,
        in_specs=placed,
        out_specs=(
            P(("replica", "mp"), None),
            P("replica", "mp"),
            P("replica", None),
            P("mp", "replica"),
            P("mp", "replica"),
            P("replica", "mp", None),
        ),
        check_vma=False,
    )
```
